32 devices in a mesh: groups: 2 (over y), ep: 4 (over z), node: 2 (over x), pair: 2 (over core).
Axes of the slice: x: 2, y: 2, z: 4, core: 2. Of those that a mesh axis runs over, the one named last changes fastest.
Arguments:
- rows_in: bfloat16 [256, 7168], P(('groups', 'ep', 'node', 'pair')), parts along dimension 0, may hold values from -6 to 6
- expert_ids: int32 [256, 2], P(('groups', 'ep', 'node', 'pair')), parts along dimension 0, may hold values from 0 to 3, all different within a row; in each aligned block of 8 rows (0 to 7, 8 to 15, ...) at most 8 rows name the same one
- gates: float32 [256, 2], P(('groups', 'ep', 'node', 'pair')), parts along dimension 0, may hold values from 0.2 to 1
- copy_expert: int32 [4], replicated, may hold values from 0 to 3, as said below
- gate_slots: bfloat16 [4, 2, 7168, 1024], P('ep', None, None, ('node', 'pair')), as said below
- up_slots: bfloat16 [4, 2, 7168, 1024], P('ep', None, None, ('node', 'pair')), as said below
- down_slots: bfloat16 [4, 2, 1024, 7168], P('ep', None, ('node', 'pair')), as said below
Outputs:
- combined: bfloat16 [256, 7168], P(('groups', 'ep', 'node', 'pair')), parts along dimension 0
The draws below stay inside these ranges and needn't reach their ends.
There are 2 independent parts, one for each index of `groups`. The reference program is written for one: setup_inputs(seed, part) draws one part's arguments, and reference() takes and returns one part's arrays. A program takes and returns all parts, laid end to end along the dimension named above; an argument that names none is the same for every part. Nothing has to cross between parts.
Inputs may be any that keep to these rules, and one draw needn't show every extreme that they name: `expert_ids`: in each aligned block of 8 rows (the rows of one device) no expert is named by more than 8 rows, and some block has an expert named by exactly 8. `copy_expert`: a permutation of the 4 experts. `gate_slots`: slot 0 of group g holds expert g; slot 1 of group g holds exactly the weights of slot 0 of group copy_expert[g]. `up_slots`: as for gate_slots. `down_slots`: as for gate_slots.
All inputs are finite; a program needn't handle non-finite values.
Results may differ from the reference program's by a relative error of at most 0.0085.
Values may be sent and summed in bfloat16 or wider, within the bound.
A program may use at most 64 MiB of HBM per device.

```python
import math
import jax
import jax.numpy as jnp
import numpy as np
from jax import lax

D = 7168
FF = 1024
TOPK = 2
ROWS_DEV = 8
EXPERTS = 4
MOST = 8
HALF = 4
ROWS = 128
N_EP = 4
N_NODE = 2
N_PAIR = 2


def copy_order(key):
    return jax.random.permutation(key, EXPERTS).astype(jnp.int32)


def paired_slots(key, order, rows_n, cols_n, fan_in):
    base = jax.random.normal(key, (EXPERTS, rows_n, cols_n), jnp.float32) * fan_in ** (-0.5)
    return jnp.stack([base, base[order]], axis=1).astype(jnp.bfloat16)


def draw_copy_expert(key, part):
    return copy_order(key)


def draw_gate_slots(key, part):
    order = copy_order(key)
    key = jax.random.fold_in(key, 1)
    return paired_slots(key, order, D, FF, D)


def draw_up_slots(key, part):
    order = copy_order(key)
    key = jax.random.fold_in(key, 2)
    return paired_slots(key, order, D, FF, D)


def draw_down_slots(key, part):
    order = copy_order(key)
    key = jax.random.fold_in(key, 3)
    return paired_slots(key, order, FF, D, FF)


def block_levels(own_key, shape, split, low, high):
    def one(dim, parts):
        draws = jax.random.uniform(jax.random.fold_in(jax.random.fold_in(own_key, 6), dim), (parts,), jnp.float32, low / len(split), high / len(split))
        return jnp.repeat(jnp.exp(draws), shape[dim] // parts).reshape((-1,) + (1,) * (len(shape) - dim - 1))

    loudness = one(*split[0])
    for cut in split[1:]:
        loudness = loudness * one(*cut)
    return loudness


def deal_out(own_key, own, number, rows, amount, top, most, skew):
    sequence = jax.random.permutation(own_key, amount)
    packed, ordinary = load_shares(amount, rows * top, most, skew, True), load_shares(amount, rows * top, most, skew, False)
    places = jnp.arange(amount)

    def named(sizes, rotation):
        used = int((sizes > 0).sum())
        fixed = max(1, used // 4)
        moved = fixed + (places - fixed + rotation * (used - fixed)) % max(1, amount - fixed)
        return jnp.zeros((amount,), jnp.int32).at[sequence[jnp.where(places < fixed, places, moved)]].set(jnp.asarray(sizes, jnp.int32))

    sizes = jnp.where(number % 4 == 0, named(packed, number // 4), named(ordinary, number - number // 4 - 1))
    mixed = jax.random.permutation(jax.random.fold_in(own, 3), amount)
    source_of, sink = mixed[0:amount // 2 * 2:2], mixed[1:amount // 2 * 2:2]
    slack = jnp.minimum(sizes[source_of] - 1, most - sizes[sink]) // 2
    slack = jnp.where((source_of == sequence[0]) | (sink == sequence[0]) | (sizes[sink] == 0), 0, jnp.maximum(slack, 0))
    moved = jax.random.randint(jax.random.fold_in(own, 4), (amount // 2,), 0, 1 << 20) % (slack + 1)
    sizes = sizes.at[source_of].add(-moved).at[sink].add(moved)
    labels = jnp.searchsorted(jnp.cumsum(sizes), jnp.arange(rows * top), side="right").astype(jnp.int32)
    table = labels.reshape(top, rows).T
    table = table[jax.random.permutation(jax.random.fold_in(own, 1), rows)]
    rotation = jax.random.randint(jax.random.fold_in(own, 2), (rows, 1), 0, top)
    return jnp.take_along_axis(table, (jnp.arange(top)[None, :] + rotation) % top, axis=1)


def load_shares(number_of, total, bound, lean, full):
    weights = [(1 << 20) // math.isqrt(rank ** lean) + 1 for rank in range(1, number_of + 1)]
    largest = bound if full else min(bound, max(-(-total // number_of), total * weights[0] // sum(weights)))
    least = 1 if total - largest >= number_of - 1 else 0
    counts, rest = [largest] + [least] * (number_of - 1), total - largest - least * (number_of - 1)
    while rest > 0:
        free = [i for i in range(1, number_of) if counts[i] < largest] or [i for i in range(1, number_of) if counts[i] < bound]
        pool, left = sum([weights[i] for i in free]), rest
        for i in free:
            more = min(bound - counts[i], max(1, left * weights[i] // pool), rest)
            counts[i] = counts[i] + more
            rest = rest - more
    return np.array(counts)


def noise(own_key, extent, scale, limit, pieces=(), kind=jnp.bfloat16):
    factor_of = block_levels(own_key, extent, pieces, -0.22, 0.18) if pieces else 1.0
    entries = jax.random.normal(own_key, extent, jnp.float32) * scale * factor_of
    return jnp.minimum(jnp.maximum(entries, -limit), limit).astype(kind)


def setup_inputs(seed: int = 0, part: int = 0) -> dict:
    seeds = jax.random.split(jax.random.key(seed), 8)
    part_splits = jax.random.split(jax.random.fold_in(seeds[7], part), 8)
    rows_in = noise(part_splits[0], (ROWS, D), 1.0, 6.0, ((0, 16),))
    expert_ids_keys = jax.random.split(jax.random.fold_in(part_splits[1], 1), ROWS // ROWS_DEV)
    expert_ids_turns = jax.random.permutation(jax.random.fold_in(part_splits[1], 3), ROWS // ROWS_DEV)
    expert_ids = jax.vmap(lambda own, number: deal_out(jax.random.fold_in(part_splits[1], 2), own, number, ROWS_DEV, EXPERTS, TOPK, MOST, 2))(expert_ids_keys, expert_ids_turns).reshape((ROWS, TOPK))
    gates = jnp.clip(jnp.exp(math.log(1.0) - 1.609438 * jax.random.uniform(part_splits[2], (ROWS, TOPK), jnp.float32) ** block_levels(part_splits[2], (ROWS, TOPK), ((0, 16),), -0.2, 0.2)), 0.2, 1.0)
    copy_expert = draw_copy_expert(jax.random.fold_in(seeds[7], 71), part)
    gate_slots = draw_gate_slots(jax.random.fold_in(seeds[7], 71), part)
    up_slots = draw_up_slots(jax.random.fold_in(seeds[7], 71), part)
    down_slots = draw_down_slots(jax.random.fold_in(seeds[7], 71), part)
    return {"rows_in": rows_in, "expert_ids": expert_ids, "gates": gates, "copy_expert": copy_expert, "gate_slots": gate_slots, "up_slots": up_slots, "down_slots": down_slots}


def swiglu_rows(inputs, gate_weight, up_weight, down_weight):
    gate_act = jnp.dot(inputs, gate_weight, preferred_element_type=jnp.float32)
    up_act = jnp.dot(inputs, up_weight, preferred_element_type=jnp.float32)
    hidden = (jax.nn.silu(gate_act) * up_act).astype(jnp.bfloat16)
    blocks = N_NODE * N_PAIR
    unit_span = hidden.shape[1] // blocks
    summed = jnp.zeros((inputs.shape[0], down_weight.shape[1]), jnp.float32)
    for section in range(blocks):
        partial_out = jnp.dot(hidden[:, section * unit_span:(section + 1) * unit_span],
                              down_weight[section * unit_span:(section + 1) * unit_span],
                              preferred_element_type=jnp.float32).astype(jnp.bfloat16)
        partial_out = lax.optimization_barrier(partial_out)
        summed = summed + partial_out.astype(jnp.float32)
    return summed


def reference(rows_in, expert_ids, gates, copy_expert, gate_slots, up_slots, down_slots):
    devices = N_EP * N_NODE * N_PAIR
    picked = expert_ids.reshape(-1).astype(jnp.int32)
    expert_list = jnp.arange(EXPERTS, dtype=jnp.int32)
    named_mask = (picked[:, None] == expert_list[None, :]).astype(jnp.int32)
    per_device = named_mask.reshape(devices, ROWS_DEV * TOPK, EXPERTS)
    earlier = jnp.cumsum(per_device, axis=1) - per_device
    ordinal = jnp.sum(earlier * per_device, axis=2).reshape(-1).astype(jnp.int32)
    holder = jnp.sum(jnp.where(copy_expert[None, :] == expert_list[:, None], expert_list[None, :], 0), axis=1).astype(jnp.int32)
    copy_group = jnp.sum(named_mask * holder[None, :], axis=1).astype(jnp.int32)
    parity = ordinal % 2
    target_group = jnp.where(parity == 0, picked, copy_group)
    location = (target_group * 2 + parity).astype(jnp.int32)
    capacity = HALF * devices
    gate_flat = gates.reshape(-1)

    def visit_slot(summed, location_id):
        chosen = location == location_id
        position = jnp.nonzero(chosen, size=capacity, fill_value=0)[0].astype(jnp.int32)
        active = jnp.arange(capacity, dtype=jnp.int32) < jnp.sum(chosen.astype(jnp.int32))
        row_index = (position // TOPK).astype(jnp.int32)
        group_id = location_id // 2
        slot_id = location_id % 2
        result = swiglu_rows(rows_in[row_index], gate_slots[group_id, slot_id],
                             up_slots[group_id, slot_id], down_slots[group_id, slot_id])
        weighting = jnp.where(active, gate_flat[position], jnp.zeros((), jnp.float32))
        return summed.at[row_index].add(weighting[:, None] * result), None

    summed, _ = lax.scan(visit_slot, jnp.zeros((ROWS, D), jnp.float32),
                         jnp.arange(2 * EXPERTS, dtype=jnp.int32))
    return summed.astype(jnp.bfloat16)
```

```python
import functools

import jax
import jax.numpy as jnp
from jax import lax
from jax.experimental import pallas as pl
from jax.experimental.pallas import tpu as pltpu
from jax.sharding import PartitionSpec as P

COLUMN_BLOCKS = 4
ROW_BLOCKS_PER_DOT = 16


def flip(a, b, size):
    if size & (size - 1):
        return lax.rem(a + b, size)
    out, bit = 0, 1
    while bit < size:
        p, q = (a // bit) % 2, (b // bit) % 2
        out = out + bit * (p + q - 2 * p * q)
        bit *= 2
    return out


def kernel(
    sizes,
    rows_ref, ids_ref, gates_ref, gate_hbm, up_hbm, down_hbm,
    out_ref,
    w_gate, w_up, w_down, rows, acc_gate, acc_up, hidden, part, part_in, node_in, sums, answers,
    w_sem, own_sem, zs, zr, xs, xr, ps, pr, ps2, pr2, xs2, xr2, zs2, zr2,
):
    n_ep, n_node, n_pair, steps = sizes
    z, x, c = lax.axis_index("ep"), lax.axis_index("node"), lax.axis_index("pair")
    blocks = rows.shape[1]
    height, cols = rows.shape[2], rows.shape[3]
    half = n_node * n_ep
    other = 1 - c
    z_order = [flip(z, s, n_ep) for s in range(n_ep)]
    x_others = [lax.rem(x + d, n_node) for d in range(1, n_node)]

    def block_of(cc, xx, zz):
        return (cc * n_node + xx) * n_ep + zz

    def remote(src, dst, send, recv, **to):
        return pltpu.make_async_remote_copy(
            src_ref=src, dst_ref=dst, send_sem=send, recv_sem=recv,
            device_id=to, device_id_type=pl.DeviceIdType.MESH,
        )

    def cut(j):
        return pl.ds(j * cols, cols)

    local = []
    for j in range(steps):
        local.append([
            pltpu.make_async_copy(gate_hbm.at[0, 0, cut(j), :], w_gate.at[j], w_sem.at[0, j]),
            pltpu.make_async_copy(up_hbm.at[0, 0, cut(j), :], w_up.at[j], w_sem.at[1, j]),
            pltpu.make_async_copy(down_hbm.at[0, 0, :, cut(j)], w_down.at[j], w_sem.at[2, j]),
            pltpu.make_async_copy(rows_ref.at[:, cut(j)], rows.at[j, block_of(c, x, z)], own_sem.at[j]),
        ])
    for j in range(steps):
        local[j][3].start()

    barrier = pltpu.get_barrier_semaphore()
    peers = [dict(ep=zz) for zz in z_order[1:]] + [dict(node=xx) for xx in x_others] + [dict(pair=other)]
    for to in peers:
        pl.semaphore_signal(barrier, inc=1, device_id=to, device_id_type=pl.DeviceIdType.MESH)
    for j in range(steps):
        for copy in local[j][:3]:
            copy.start()
    pl.semaphore_wait(barrier, len(peers))

    sends = []

    def go(copy):
        copy.start()
        sends.append(copy)

    def own_out(j):
        mine = rows_ref.at[:, cut(j)]
        slot = rows.at[j, block_of(c, x, z)]
        for zz in reversed(z_order[1:]):
            go(remote(mine, slot, zs.at[j, zz], zr.at[j, z], ep=zz))
        for xx in x_others:
            go(remote(mine, slot, xs.at[j, z, xx], xr.at[j, z, x], node=xx))

    def forward_nodes(j):
        for zz in z_order[1:]:
            slot = rows.at[j, block_of(c, x, zz)]
            remote(slot, slot, zs.at[j, zz], zr.at[j, zz], ep=zz).wait_recv()
            for xx in x_others:
                go(remote(slot, slot, xs.at[j, zz, xx], xr.at[j, zz, x], node=xx))

    def forward_pair(j):
        for zz in z_order:
            for xx in x_others:
                slot = rows.at[j, block_of(c, xx, zz)]
                remote(slot, slot, xs.at[j, zz, xx], xr.at[j, zz, xx], node=xx).wait_recv()
        local[j][3].wait()
        mine = rows.at[j, pl.ds(c * half, half)]
        go(remote(mine, mine, ps.at[j], pr.at[j], pair=other))

    group = min(ROW_BLOCKS_PER_DOT, blocks)

    def tiles(body):
        if blocks == group:
            body(0)
        else:
            lax.fori_loop(0, blocks // group, lambda i, _: (body(i), 0)[1], 0)

    def into(j):
        theirs = rows.at[j, pl.ds(other * half, half)]
        remote(theirs, theirs, ps.at[j], pr.at[j], pair=other).wait_recv()
        local[j][0].wait()
        local[j][1].wait()

        def body(i):
            data = rows[j, pl.ds(i * group, group)].astype(jnp.float32)
            data = data.reshape(group * height, cols).astype(jnp.bfloat16)
            for acc, weight in ((acc_gate, w_gate), (acc_up, w_up)):
                value = jnp.dot(data, weight[j], preferred_element_type=jnp.float32)
                if j == 0:
                    acc[i] = value
                else:
                    acc[i] += value
        tiles(body)

    def activate():
        def body(i):
            gate = acc_gate[i]
            hidden[i] = (gate / (1.0 + jnp.exp(-gate)) * acc_up[i]).astype(jnp.bfloat16)
        tiles(body)

    def down(j):
        local[j][2].wait()

        def body(i):
            value = jnp.dot(hidden[i], w_down[j], preferred_element_type=jnp.float32)
            part[j, pl.ds(i * group, group)] = value.reshape(group, height, cols).astype(jnp.bfloat16)
        tiles(body)
        go(remote(part.at[j, pl.ds(other * half, half)], part_in.at[j], ps2.at[j], pr2.at[j], pair=other))

    def sum_pair(j):
        remote(part_in.at[j], part_in.at[j], ps2.at[j], pr2.at[j], pair=other).wait_recv()
        for xx in x_others + [x]:
            here = pl.ds(xx * n_ep, n_ep)
            mine = part[j, pl.ds(c * half + xx * n_ep, n_ep)].astype(jnp.float32)
            part_in[j, here] = (part_in[j, here].astype(jnp.float32) + mine).astype(jnp.bfloat16)
        for xx in x_others:
            go(remote(part_in.at[j, pl.ds(xx * n_ep, n_ep)], node_in.at[j, x],
                      xs2.at[j, xx], xr2.at[j, x], node=xx))

    def sum_nodes(j):
        total = part_in[j, pl.ds(x * n_ep, n_ep)].astype(jnp.float32)
        for xx in x_others:
            slot = node_in.at[j, xx]
            remote(slot, slot, xs2.at[j, xx], xr2.at[j, xx], node=xx).wait_recv()
            total = total + node_in[j, xx].astype(jnp.float32)
        sums[j] = total.astype(jnp.bfloat16)
        for zz in reversed(z_order[1:]):
            go(remote(sums.at[j, zz], answers.at[j, z], zs2.at[j, zz], zr2.at[j, z], ep=zz))

    def weight_of(zz):
        return jnp.sum(jnp.where(ids_ref[...] == zz, gates_ref[...], 0.0), axis=1, keepdims=True)

    def finish(j):
        total = None
        for zz in z_order:
            if zz is z_order[0]:
                value = sums[j, zz].astype(jnp.float32)
            else:
                slot = answers.at[j, zz]
                remote(slot, slot, zs2.at[j, zz], zr2.at[j, zz], ep=zz).wait_recv()
                value = answers[j, zz].astype(jnp.float32)
            share = weight_of(zz)
            value = jnp.where(share > 0.0, share * value, 0.0)
            total = value if total is None else total + value
        out_ref[:, cut(j)] = total.astype(jnp.bfloat16)

    for j in range(steps):
        own_out(j)
    for t in range(steps + 2):
        if t < steps:
            forward_nodes(t)
        if 0 <= t - 1 < steps:
            forward_pair(t - 1)
        if 0 <= t - 2 < steps:
            into(t - 2)
    activate()
    for t in range(steps + 1):
        if t < steps:
            down(t)
        if t >= 1:
            sum_pair(t - 1)
    for j in range(steps):
        sum_nodes(j)
    for j in range(steps):
        finish(j)
    for copy in sends:
        copy.wait_send()


def solution(mesh):
    n_ep, n_node, n_pair = (mesh.shape[name] for name in ("ep", "node", "pair"))
    steps = COLUMN_BLOCKS

    def per_device(rows_in, expert_ids, gates, copy_expert, gate_slots, up_slots, down_slots):
        height, width = rows_in.shape
        units = gate_slots.shape[3]
        cols = width // steps
        blocks = n_ep * n_node * n_pair
        group = min(ROW_BLOCKS_PER_DOT, blocks)
        bf16, f32 = jnp.bfloat16, jnp.float32
        dma = pltpu.SemaphoreType.DMA
        anywhere = pl.BlockSpec(memory_space=pl.ANY)
        vmem = pl.BlockSpec(memory_space=pltpu.VMEM)
        return pl.pallas_call(
            functools.partial(kernel, (n_ep, n_node, n_pair, steps)),
            out_shape=jax.ShapeDtypeStruct((height, width), bf16),
            in_specs=[anywhere, vmem, vmem, anywhere, anywhere, anywhere],
            out_specs=vmem,
            scratch_shapes=[
                pltpu.VMEM((steps, cols, units), bf16),
                pltpu.VMEM((steps, cols, units), bf16),
                pltpu.VMEM((steps, units, cols), bf16),
                pltpu.VMEM((steps, blocks, height, cols), bf16),
                pltpu.VMEM((blocks // group, group * height, units), f32),
                pltpu.VMEM((blocks // group, group * height, units), f32),
                pltpu.VMEM((blocks // group, group * height, units), bf16),
                pltpu.VMEM((steps, blocks, height, cols), bf16),
                pltpu.VMEM((steps, n_ep * n_node, height, cols), bf16),
                pltpu.VMEM((steps, n_node, n_ep, height, cols), bf16),
                pltpu.VMEM((steps, n_ep, height, cols), bf16),
                pltpu.VMEM((steps, n_ep, height, cols), bf16),
                dma((3, steps)), dma((steps,)),
                dma((steps, n_ep)), dma((steps, n_ep)),
                dma((steps, n_ep, n_node)), dma((steps, n_ep, n_node)),
                dma((steps,)), dma((steps,)),
                dma((steps,)), dma((steps,)),
                dma((steps, n_node)), dma((steps, n_node)),
                dma((steps, n_ep)), dma((steps, n_ep)),
            ],
            compiler_params=pltpu.CompilerParams(
                collective_id=0, has_side_effects=True, vmem_limit_bytes=60 * 1024 * 1024
            ),
        )(rows_in, expert_ids, gates, gate_slots, up_slots, down_slots)

    spec = P(("groups", "ep", "node", "pair"), None)
    return jax.shard_map(
        per_device,
        mesh=mesh,
        in_specs=(
            spec, spec, spec, P(),
            P("ep", None, None, ("node", "pair")),
            P("ep", None, None, ("node", "pair")),
            P("ep", None, ("node", "pair"), None),
        ),
        out_specs=spec,
        check_vma=False,
    )
```

```python
import functools

import jax
import jax.numpy as jnp
from jax import lax
from jax.experimental import pallas as pl
from jax.experimental.pallas import tpu as pltpu
from jax.sharding import PartitionSpec as P

COLUMN_BLOCKS = 4
AHEAD = 2
ROW_BLOCKS_PER_DOT = 16


def flip(a, b, size):
    if size & (size - 1):
        return lax.rem(a + b, size)
    out, bit = 0, 1
    while bit < size:
        p, q = (a // bit) % 2, (b // bit) % 2
        out = out + bit * (p + q - 2 * p * q)
        bit *= 2
    return out


def kernel(
    sizes,
    rows_ref, ids_ref, gates_ref, gate_hbm, up_hbm, down_hbm,
    out_ref,
    w_gate, w_up, w_down, rows, acc_gate, acc_up, hidden, part, part_in, node_in, sums, answers,
    w_sem, own_sem, zs, zr, xs, xr, ps, pr, ps2, pr2, xs2, xr2, zs2, zr2,
):
    n_ep, n_node, n_pair, steps = sizes
    z, x, c = lax.axis_index("ep"), lax.axis_index("node"), lax.axis_index("pair")
    blocks = rows.shape[1]
    height, cols = rows.shape[2], rows.shape[3]
    half = n_node * n_ep
    other = 1 - c
    z_order = [flip(z, s, n_ep) for s in range(n_ep)]
    x_others = [lax.rem(x + d, n_node) for d in range(1, n_node)]

    def block_of(cc, xx, zz):
        return (cc * n_node + xx) * n_ep + zz

    def remote(src, dst, send, recv, **to):
        return pltpu.make_async_remote_copy(
            src_ref=src, dst_ref=dst, send_sem=send, recv_sem=recv,
            device_id=to, device_id_type=pl.DeviceIdType.MESH,
        )

    def cut(j):
        return pl.ds(j * cols, cols)

    local = []
    for j in range(steps):
        local.append([
            pltpu.make_async_copy(gate_hbm.at[0, 0, cut(j), :], w_gate.at[j], w_sem.at[0, j]),
            pltpu.make_async_copy(up_hbm.at[0, 0, cut(j), :], w_up.at[j], w_sem.at[1, j]),
            pltpu.make_async_copy(down_hbm.at[0, 0, :, cut(j)], w_down.at[j], w_sem.at[2, j]),
            pltpu.make_async_copy(rows_ref.at[:, cut(j)], rows.at[j, block_of(c, x, z)], own_sem.at[j]),
        ])
    for j in range(steps):
        local[j][3].start()

    barrier = pltpu.get_barrier_semaphore()
    peers = [dict(ep=zz) for zz in z_order[1:]] + [dict(node=xx) for xx in x_others] + [dict(pair=other)]
    for to in peers:
        pl.semaphore_signal(barrier, inc=1, device_id=to, device_id_type=pl.DeviceIdType.MESH)
    for j in range(steps):
        for copy in local[j][:3]:
            copy.start()
    pl.semaphore_wait(barrier, len(peers))

    sends = []

    def go(copy):
        copy.start()
        sends.append(copy)

    def own_out(j):
        mine = rows_ref.at[:, cut(j)]
        slot = rows.at[j, block_of(c, x, z)]
        for zz in z_order[1:]:
            go(remote(mine, slot, zs.at[j, zz], zr.at[j, z], ep=zz))
        for xx in x_others:
            go(remote(mine, slot, xs.at[j, z, xx], xr.at[j, z, x], node=xx))

    def forward_nodes(j):
        for zz in z_order[1:]:
            slot = rows.at[j, block_of(c, x, zz)]
            remote(slot, slot, zs.at[j, zz], zr.at[j, zz], ep=zz).wait_recv()
            for xx in x_others:
                go(remote(slot, slot, xs.at[j, zz, xx], xr.at[j, zz, x], node=xx))

    def forward_pair(j):
        for zz in z_order:
            for xx in x_others:
                slot = rows.at[j, block_of(c, xx, zz)]
                remote(slot, slot, xs.at[j, zz, xx], xr.at[j, zz, xx], node=xx).wait_recv()
        local[j][3].wait()
        mine = rows.at[j, pl.ds(c * half, half)]
        go(remote(mine, mine, ps.at[j], pr.at[j], pair=other))

    group = min(ROW_BLOCKS_PER_DOT, blocks)

    def tiles(body):
        if blocks == group:
            body(0)
        else:
            lax.fori_loop(0, blocks // group, lambda i, _: (body(i), 0)[1], 0)

    def into(j):
        theirs = rows.at[j, pl.ds(other * half, half)]
        remote(theirs, theirs, ps.at[j], pr.at[j], pair=other).wait_recv()
        local[j][0].wait()
        local[j][1].wait()

        def body(i):
            data = rows[j, pl.ds(i * group, group)].astype(jnp.float32)
            data = data.reshape(group * height, cols).astype(jnp.bfloat16)
            for acc, weight in ((acc_gate, w_gate), (acc_up, w_up)):
                value = jnp.dot(data, weight[j], preferred_element_type=jnp.float32)
                if j == 0:
                    acc[i] = value
                else:
                    acc[i] += value
        tiles(body)

    def activate():
        def body(i):
            gate = acc_gate[i]
            hidden[i] = (gate / (1.0 + jnp.exp(-gate)) * acc_up[i]).astype(jnp.bfloat16)
        tiles(body)

    def down(j):
        local[j][2].wait()

        def body(i):
            value = jnp.dot(hidden[i], w_down[j], preferred_element_type=jnp.float32)
            part[j, pl.ds(i * group, group)] = value.reshape(group, height, cols).astype(jnp.bfloat16)
        tiles(body)
        go(remote(part.at[j, pl.ds(other * half, half)], part_in.at[j], ps2.at[j], pr2.at[j], pair=other))

    def sum_pair(j):
        remote(part_in.at[j], part_in.at[j], ps2.at[j], pr2.at[j], pair=other).wait_recv()
        for xx in x_others + [x]:
            here = pl.ds(xx * n_ep, n_ep)
            mine = part[j, pl.ds(c * half + xx * n_ep, n_ep)].astype(jnp.float32)
            part_in[j, here] = (part_in[j, here].astype(jnp.float32) + mine).astype(jnp.bfloat16)

    def send_nodes(j):
        for xx in x_others:
            go(remote(part_in.at[j, pl.ds(xx * n_ep, n_ep)], node_in.at[j, x],
                      xs2.at[j, xx], xr2.at[j, x], node=xx))

    def sum_nodes(j):
        total = part_in[j, pl.ds(x * n_ep, n_ep)].astype(jnp.float32)
        for xx in x_others:
            slot = node_in.at[j, xx]
            remote(slot, slot, xs2.at[j, xx], xr2.at[j, xx], node=xx).wait_recv()
            total = total + node_in[j, xx].astype(jnp.float32)
        sums[j] = total.astype(jnp.bfloat16)
        for zz in z_order[1:]:
            go(remote(sums.at[j, zz], answers.at[j, z], zs2.at[j, zz], zr2.at[j, z], ep=zz))

    def weight_of(zz):
        named = jnp.sum(jnp.where(ids_ref[...] == zz, gates_ref[...], 0.0), axis=0, keepdims=True)
        square = (height, height)
        diagonal = lax.broadcasted_iota(jnp.int32, square, 0) == lax.broadcasted_iota(jnp.int32, square, 1)
        return jnp.sum(jnp.where(diagonal, jnp.broadcast_to(named, square), 0.0), axis=1, keepdims=True)

    def finish(j):
        total = None
        for zz in z_order:
            if zz is z_order[0]:
                value = sums[j, zz].astype(jnp.float32)
            else:
                slot = answers.at[j, zz]
                remote(slot, slot, zs2.at[j, zz], zr2.at[j, zz], ep=zz).wait_recv()
                value = answers[j, zz].astype(jnp.float32)
            share = weight_of(zz)
            value = jnp.where(share > 0.0, share * value, 0.0)
            total = value if total is None else total + value
        out_ref[:, cut(j)] = total.astype(jnp.bfloat16)

    ahead = min(AHEAD, steps)
    for j in range(ahead):
        own_out(j)
    for t in range(steps + 2):
        if t < steps:
            forward_nodes(t)
        if t + ahead < steps:
            own_out(t + ahead)
        if 0 <= t - 1 < steps:
            forward_pair(t - 1)
        if 0 <= t - 2 < steps:
            into(t - 2)
    activate()
    for t in range(steps + 1):
        if t < steps:
            down(t)
        if t >= 1:
            sum_pair(t - 1)
            if t - 1 < ahead:
                send_nodes(t - 1)
    for t in range(steps + 2):
        if t < steps:
            sum_nodes(t)
        if t + ahead < steps:
            send_nodes(t + ahead)
        if t >= 2:
            finish(t - 2)
    for copy in sends:
        copy.wait_send()


def solution(mesh):
    n_ep, n_node, n_pair = (mesh.shape[name] for name in ("ep", "node", "pair"))
    steps = COLUMN_BLOCKS

    def per_device(rows_in, expert_ids, gates, copy_expert, gate_slots, up_slots, down_slots):
        height, width = rows_in.shape
        units = gate_slots.shape[3]
        cols = width // steps
        blocks = n_ep * n_node * n_pair
        group = min(ROW_BLOCKS_PER_DOT, blocks)
        bf16, f32 = jnp.bfloat16, jnp.float32
        dma = pltpu.SemaphoreType.DMA
        anywhere = pl.BlockSpec(memory_space=pl.ANY)
        vmem = pl.BlockSpec(memory_space=pltpu.VMEM)
        return pl.pallas_call(
            functools.partial(kernel, (n_ep, n_node, n_pair, steps)),
            out_shape=jax.ShapeDtypeStruct((height, width), bf16),
            in_specs=[anywhere, vmem, vmem, anywhere, anywhere, anywhere],
            out_specs=vmem,
            scratch_shapes=[
                pltpu.VMEM((steps, cols, units), bf16),
                pltpu.VMEM((steps, cols, units), bf16),
                pltpu.VMEM((steps, units, cols), bf16),
                pltpu.VMEM((steps, blocks, height, cols), bf16),
                pltpu.VMEM((blocks // group, group * height, units), f32),
                pltpu.VMEM((blocks // group, group * height, units), f32),
                pltpu.VMEM((blocks // group, group * height, units), bf16),
                pltpu.VMEM((steps, blocks, height, cols), bf16),
                pltpu.VMEM((steps, n_ep * n_node, height, cols), bf16),
                pltpu.VMEM((steps, n_node, n_ep, height, cols), bf16),
                pltpu.VMEM((steps, n_ep, height, cols), bf16),
                pltpu.VMEM((steps, n_ep, height, cols), bf16),
                dma((3, steps)), dma((steps,)),
                dma((steps, n_ep)), dma((steps, n_ep)),
                dma((steps, n_ep, n_node)), dma((steps, n_ep, n_node)),
                dma((steps,)), dma((steps,)),
                dma((steps,)), dma((steps,)),
                dma((steps, n_node)), dma((steps, n_node)),
                dma((steps, n_ep)), dma((steps, n_ep)),
            ],
            compiler_params=pltpu.CompilerParams(
                collective_id=0, has_side_effects=True, vmem_limit_bytes=60 * 1024 * 1024
            ),
        )(rows_in, expert_ids.T, gates.T, gate_slots, up_slots, down_slots)

    spec = P(("groups", "ep", "node", "pair"), None)
    return jax.shard_map(
        per_device,
        mesh=mesh,
        in_specs=(
            spec, spec, spec, P(),
            P("ep", None, None, ("node", "pair")),
            P("ep", None, None, ("node", "pair")),
            P("ep", None, ("node", "pair"), None),
        ),
        out_specs=spec,
        check_vma=False,
    )
```

```python
import functools

import jax
import jax.numpy as jnp
from jax import lax
from jax.experimental import pallas as pl
from jax.experimental.pallas import tpu as pltpu
from jax.sharding import PartitionSpec as P

GATHER_SPLIT = (14, 14, 14, 14)
RETURN_SPLIT = (14, 14, 14, 14)
GATHER_AHEAD = 2
RETURN_AHEAD = 2
ROW_BLOCKS_PER_DOT = 16


def flip(a, b, size):
    if size & (size - 1):
        return lax.rem(a + b, size)
    out, bit = 0, 1
    while bit < size:
        p, q = (a // bit) % 2, (b // bit) % 2
        out = out + bit * (p + q - 2 * p * q)
        bit *= 2
    return out


def kernel(
    sizes,
    rows_ref, ids_hbm, gates_hbm, gate_hbm, up_hbm, down_hbm,
    out_hbm,
    ids_ref, gates_ref, out_ref, w_gate, w_up, w_down, rows, acc_gate, acc_up, hidden, part, part_in, node_in, sums, answers,
    w_sem, own_sem, out_sem, zs, zr, xs, xr, ps, pr, ps2, pr2, xs2, xr2, zs2, zr2,
):
    n_ep, n_node, n_pair = sizes
    z, x, c = lax.axis_index("ep"), lax.axis_index("node"), lax.axis_index("pair")
    blocks, height = rows.shape[0], rows.shape[1]
    half = n_node * n_ep
    other = 1 - c
    z_order = [flip(z, s, n_ep) for s in range(n_ep)]
    x_others = [lax.rem(x + d, n_node) for d in range(1, n_node)]

    def block_of(cc, xx, zz):
        return (cc * n_node + xx) * n_ep + zz

    def remote(src, dst, send, recv, **to):
        return pltpu.make_async_remote_copy(
            src_ref=src, dst_ref=dst, send_sem=send, recv_sem=recv,
            device_id=to, device_id_type=pl.DeviceIdType.MESH,
        )

    def cut_in(j):
        return pl.ds(sum(GATHER_SPLIT[:j]) * 128, GATHER_SPLIT[j] * 128)

    def cut_out(j):
        return pl.ds(sum(RETURN_SPLIT[:j]) * 128, RETURN_SPLIT[j] * 128)

    steps, steps_out = len(GATHER_SPLIT), len(RETURN_SPLIT)

    own = rows.at[block_of(c, x, z)]
    own_copy = pltpu.make_async_copy(rows_ref, own, own_sem.at[0])
    own_copy.start()
    ids_copy = pltpu.make_async_copy(ids_hbm, ids_ref, own_sem.at[1])
    gates_copy = pltpu.make_async_copy(gates_hbm, gates_ref, own_sem.at[2])
    outs = [
        pltpu.make_async_copy(out_ref.at[:, cut_out(j)], out_hbm.at[:, cut_out(j)], out_sem.at[j])
        for j in range(steps_out)
    ]
    weights_in = [
        [pltpu.make_async_copy(gate_hbm.at[0, 0, cut_in(j), :], w_gate.at[cut_in(j), :], w_sem.at[0, j]),
         pltpu.make_async_copy(up_hbm.at[0, 0, cut_in(j), :], w_up.at[cut_in(j), :], w_sem.at[1, j])]
        for j in range(steps)
    ]
    weights_out = [
        pltpu.make_async_copy(down_hbm.at[0, 0, :, cut_out(j)], w_down.at[:, cut_out(j)], w_sem.at[2, j])
        for j in range(steps_out)
    ]

    barrier = pltpu.get_barrier_semaphore()
    peers = [dict(ep=zz) for zz in z_order[1:]] + [dict(node=xx) for xx in x_others] + [dict(pair=other)]
    for to in peers:
        pl.semaphore_signal(barrier, inc=1, device_id=to, device_id_type=pl.DeviceIdType.MESH)
    for copy in sum(weights_in, []) + weights_out:
        copy.start()
    ids_copy.start()
    gates_copy.start()
    pl.semaphore_wait(barrier, len(peers))

    sends = []

    def go(copy):
        copy.start()
        sends.append(copy)

    def own_out(j):
        slot = rows.at[block_of(c, x, z), :, cut_in(j)]
        for zz in z_order[1:]:
            go(remote(slot, slot, zs.at[j, zz], zr.at[j, z], ep=zz))

    def own_nodes():
        slot = own
        for xx in x_others:
            go(remote(slot, slot, xs.at[0, z, xx], xr.at[0, z, x], node=xx))

    def forward_nodes(j):
        for zz in z_order[1:]:
            slot = rows.at[block_of(c, x, zz), :, cut_in(j)]
            remote(slot, slot, zs.at[j, zz], zr.at[j, zz], ep=zz).wait_recv()
            for xx in x_others:
                go(remote(slot, slot, xs.at[j, zz, xx], xr.at[j, zz, x], node=xx))

    def forward_pair(j):
        for zz in z_order[1:] if j else z_order:
            for xx in x_others:
                slot = rows.at[block_of(c, xx, zz), :, cut_in(j) if zz is not z_order[0] else slice(None)]
                remote(slot, slot, xs.at[j, zz, xx], xr.at[j, zz, xx], node=xx).wait_recv()
        mine = rows.at[pl.ds(c * half, half), :, cut_in(j)]
        go(remote(mine, mine, ps.at[j], pr.at[j], pair=other))

    group = min(ROW_BLOCKS_PER_DOT, blocks)

    def tiles(body):
        if blocks == group:
            body(0)
        else:
            lax.fori_loop(0, blocks // group, lambda i, _: (body(i), 0)[1], 0)

    def into(j):
        theirs = rows.at[pl.ds(other * half, half), :, cut_in(j)]
        remote(theirs, theirs, ps.at[j], pr.at[j], pair=other).wait_recv()
        for copy in weights_in[j]:
            copy.wait()

        def body(i):
            data = rows[pl.ds(i * group, group), :, cut_in(j)].astype(jnp.float32)
            data = data.reshape(group * height, GATHER_SPLIT[j] * 128).astype(jnp.bfloat16)
            for acc, weight in ((acc_gate, w_gate), (acc_up, w_up)):
                value = jnp.dot(data, weight[cut_in(j), :], preferred_element_type=jnp.float32)
                if j == 0:
                    acc[i] = value
                else:
                    acc[i] += value
        tiles(body)

    def activate():
        def body(i):
            gate = acc_gate[i]
            hidden[i] = (gate / (1.0 + jnp.exp(-gate)) * acc_up[i]).astype(jnp.bfloat16)
        tiles(body)

    def down(j):
        weights_out[j].wait()

        def body(i):
            value = jnp.dot(hidden[i], w_down[:, cut_out(j)], preferred_element_type=jnp.float32)
            part[pl.ds(i * group, group), :, cut_out(j)] = value.reshape(group, height, RETURN_SPLIT[j] * 128).astype(jnp.bfloat16)
        tiles(body)
        go(remote(part.at[pl.ds(other * half, half), :, cut_out(j)], part_in.at[:, :, cut_out(j)], ps2.at[j], pr2.at[j], pair=other))

    def sum_pair(j):
        remote(part_in.at[:, :, cut_out(j)], part_in.at[:, :, cut_out(j)], ps2.at[j], pr2.at[j], pair=other).wait_recv()
        for xx in x_others:
            here = pl.ds(xx * n_ep, n_ep)
            mine = part[pl.ds(c * half + xx * n_ep, n_ep), :, cut_out(j)].astype(jnp.float32)
            part_in[here, :, cut_out(j)] = (part_in[here, :, cut_out(j)].astype(jnp.float32) + mine).astype(jnp.bfloat16)

    def send_nodes(j):
        for xx in x_others:
            go(remote(part_in.at[pl.ds(xx * n_ep, n_ep), :, cut_out(j)], node_in.at[x, :, :, cut_out(j)],
                      xs2.at[j, xx], xr2.at[j, x], node=xx))

    def sum_nodes(j):
        total = part_in[pl.ds(x * n_ep, n_ep), :, cut_out(j)].astype(jnp.float32)
        total = total + part[pl.ds(c * half + x * n_ep, n_ep), :, cut_out(j)].astype(jnp.float32)
        for xx in x_others:
            slot = node_in.at[xx, :, :, cut_out(j)]
            remote(slot, slot, xs2.at[j, xx], xr2.at[j, xx], node=xx).wait_recv()
            total = total + node_in[xx, :, :, cut_out(j)].astype(jnp.float32)
        sums[:, :, cut_out(j)] = total.astype(jnp.bfloat16)
        for zz in z_order[1:]:
            go(remote(sums.at[zz, :, cut_out(j)], answers.at[z, :, cut_out(j)], zs2.at[j, zz], zr2.at[j, z], ep=zz))

    def weight_of(zz):
        named = jnp.sum(jnp.where(ids_ref[...] == zz, gates_ref[...], 0.0), axis=0, keepdims=True)
        square = (height, height)
        diagonal = lax.broadcasted_iota(jnp.int32, square, 0) == lax.broadcasted_iota(jnp.int32, square, 1)
        return jnp.sum(jnp.where(diagonal, jnp.broadcast_to(named, square), 0.0), axis=1, keepdims=True)

    def finish(j):
        total = None
        for zz in z_order:
            if zz is z_order[0]:
                value = sums[zz, :, cut_out(j)].astype(jnp.float32)
            else:
                slot = answers.at[zz, :, cut_out(j)]
                remote(slot, slot, zs2.at[j, zz], zr2.at[j, zz], ep=zz).wait_recv()
                value = answers[zz, :, cut_out(j)].astype(jnp.float32)
            share = weight_of(zz)
            value = jnp.where(share > 0.0, share * value, 0.0)
            total = value if total is None else total + value
        out_ref[:, cut_out(j)] = total.astype(jnp.bfloat16)
        outs[j].start()

    def drain():
        while sends:
            sends.pop(0).wait_send()

    own_copy.wait()
    ahead = min(GATHER_AHEAD, steps)
    for j in range(ahead):
        own_out(j)
        if j == 0:
            own_nodes()
    ahead_back = min(RETURN_AHEAD, steps_out)
    for t in range(steps + 2):
        if t < steps:
            forward_nodes(t)
        if t + ahead < steps:
            own_out(t + ahead)
        if 0 <= t - 1 < steps:
            forward_pair(t - 1)
        if 0 <= t - 2 < steps:
            into(t - 2)
    activate()
    ids_copy.wait()
    gates_copy.wait()
    for t in range(steps_out + 1):
        if t < steps_out:
            down(t)
        if t >= 1:
            sum_pair(t - 1)
            if t - 1 < ahead_back:
                send_nodes(t - 1)
    drain()
    for t in range(steps_out + 2):
        if t < steps_out:
            sum_nodes(t)
        if t + ahead_back < steps_out:
            send_nodes(t + ahead_back)
        if t >= 2:
            finish(t - 2)
    drain()
    for copy in outs:
        copy.wait()


def solution(mesh):
    n_ep, n_node, n_pair = (mesh.shape[name] for name in ("ep", "node", "pair"))
    steps = max(len(GATHER_SPLIT), len(RETURN_SPLIT))

    def per_device(rows_in, expert_ids, gates, copy_expert, gate_slots, up_slots, down_slots):
        height, width = rows_in.shape
        units = gate_slots.shape[3]
        blocks = n_ep * n_node * n_pair
        group = min(ROW_BLOCKS_PER_DOT, blocks)
        bf16, f32 = jnp.bfloat16, jnp.float32
        dma = pltpu.SemaphoreType.DMA
        anywhere = pl.BlockSpec(memory_space=pl.ANY)
        return pl.pallas_call(
            functools.partial(kernel, (n_ep, n_node, n_pair)),
            out_shape=jax.ShapeDtypeStruct((height, width), bf16),
            in_specs=[anywhere] * 6,
            out_specs=anywhere,
            scratch_shapes=[
                pltpu.VMEM(expert_ids.T.shape, jnp.int32),
                pltpu.VMEM(gates.T.shape, f32),
                pltpu.VMEM((height, width), bf16),
                pltpu.VMEM((width, units), bf16),
                pltpu.VMEM((width, units), bf16),
                pltpu.VMEM((units, width), bf16),
                pltpu.VMEM((blocks, height, width), bf16),
                pltpu.VMEM((blocks // group, group * height, units), f32),
                pltpu.VMEM((blocks // group, group * height, units), f32),
                pltpu.VMEM((blocks // group, group * height, units), bf16),
                pltpu.VMEM((blocks, height, width), bf16),
                pltpu.VMEM((n_ep * n_node, height, width), bf16),
                pltpu.VMEM((n_node, n_ep, height, width), bf16),
                pltpu.VMEM((n_ep, height, width), bf16),
                pltpu.VMEM((n_ep, height, width), bf16),
                dma((3, steps)), dma((3,)), dma((steps,)),
                dma((steps, n_ep)), dma((steps, n_ep)),
                dma((steps, n_ep, n_node)), dma((steps, n_ep, n_node)),
                dma((steps,)), dma((steps,)),
                dma((steps,)), dma((steps,)),
                dma((steps, n_node)), dma((steps, n_node)),
                dma((steps, n_ep)), dma((steps, n_ep)),
            ],
            compiler_params=pltpu.CompilerParams(
                collective_id=0, has_side_effects=True, vmem_limit_bytes=60 * 1024 * 1024
            ),
        )(rows_in, expert_ids.T, gates.T, gate_slots, up_slots, down_slots)

    spec = P(("groups", "ep", "node", "pair"), None)
    return jax.shard_map(
        per_device,
        mesh=mesh,
        in_specs=(
            spec, spec, spec, P(),
            P("ep", None, None, ("node", "pair")),
            P("ep", None, None, ("node", "pair")),
            P("ep", None, ("node", "pair"), None),
        ),
        out_specs=spec,
        check_vma=False,
    )
```

```python
import functools

import jax
import jax.numpy as jnp
from jax import lax
from jax.experimental import pallas as pl
from jax.experimental.pallas import tpu as pltpu
from jax.sharding import PartitionSpec as P

GATHER_SPLIT = (14, 14, 14, 14)
RETURN_SPLIT = (14, 14, 14, 14)
GATHER_AHEAD = 2
RETURN_AHEAD = 2
ROW_BLOCKS_PER_DOT = 16


def flip(a, b, size):
    if size & (size - 1):
        return lax.rem(a + b, size)
    out, bit = 0, 1
    while bit < size:
        p, q = (a // bit) % 2, (b // bit) % 2
        out = out + bit * (p + q - 2 * p * q)
        bit *= 2
    return out


def kernel(
    sizes,
    rows_ref, ids_hbm, gates_hbm, gate_hbm, up_hbm, down_hbm,
    out_hbm,
    ids_ref, gates_ref, out_ref, w_gate, w_up, w_down, rows, acc_gate, acc_up, hidden, part, part_in, node_in, sums, answers,
    w_sem, own_sem, out_sem, zs, zr, xs, xr, ps, pr, ps2, pr2, xs2, xr2, zs2, zr2,
):
    n_ep, n_node, n_pair = sizes
    z, x, c = lax.axis_index("ep"), lax.axis_index("node"), lax.axis_index("pair")
    blocks, height = rows.shape[0], rows.shape[1]
    half = n_node * n_ep
    other = 1 - c
    z_order = [flip(z, s, n_ep) for s in range(n_ep)]
    x_others = [lax.rem(x + d, n_node) for d in range(1, n_node)]

    def block_of(cc, xx, zz):
        return (cc * n_node + xx) * n_ep + zz

    def remote(src, dst, send, recv, **to):
        return pltpu.make_async_remote_copy(
            src_ref=src, dst_ref=dst, send_sem=send, recv_sem=recv,
            device_id=to, device_id_type=pl.DeviceIdType.MESH,
        )

    def cut_in(j):
        return pl.ds(sum(GATHER_SPLIT[:j]) * 128, GATHER_SPLIT[j] * 128)

    def cut_out(j):
        return pl.ds(sum(RETURN_SPLIT[:j]) * 128, RETURN_SPLIT[j] * 128)

    steps, steps_out = len(GATHER_SPLIT), len(RETURN_SPLIT)

    own = rows.at[block_of(c, x, z)]
    own_copy = pltpu.make_async_copy(rows_ref, own, own_sem.at[0])
    own_copy.start()
    ids_copy = pltpu.make_async_copy(ids_hbm, ids_ref, own_sem.at[1])
    gates_copy = pltpu.make_async_copy(gates_hbm, gates_ref, own_sem.at[2])
    outs = [
        pltpu.make_async_copy(out_ref.at[:, cut_out(j)], out_hbm.at[:, cut_out(j)], out_sem.at[j])
        for j in range(steps_out)
    ]
    weights_in = [
        [pltpu.make_async_copy(gate_hbm.at[0, 0, cut_in(j), :], w_gate.at[cut_in(j), :], w_sem.at[0, j]),
         pltpu.make_async_copy(up_hbm.at[0, 0, cut_in(j), :], w_up.at[cut_in(j), :], w_sem.at[1, j])]
        for j in range(steps)
    ]
    weights_out = [
        pltpu.make_async_copy(down_hbm.at[0, 0, :, cut_out(j)], w_down.at[:, cut_out(j)], w_sem.at[2, j])
        for j in range(steps_out)
    ]

    barrier = pltpu.get_barrier_semaphore()
    peers = [dict(ep=zz) for zz in z_order[1:]] + [dict(node=xx) for xx in x_others] + [dict(pair=other)]
    for to in peers:
        pl.semaphore_signal(barrier, inc=1, device_id=to, device_id_type=pl.DeviceIdType.MESH)
    ids_copy.start()
    gates_copy.start()
    pl.semaphore_wait(barrier, len(peers))

    sends = []

    def go(copy):
        copy.start()
        sends.append(copy)

    def own_out(j):
        slot = rows.at[block_of(c, x, z), :, cut_in(j)]
        for zz in z_order[1:]:
            go(remote(slot, slot, zs.at[j, zz], zr.at[j, z], ep=zz))

    def own_nodes():
        slot = own
        for xx in x_others:
            go(remote(slot, slot, xs.at[0, z, xx], xr.at[0, z, x], node=xx))

    def forward_nodes(j):
        for zz in z_order[1:]:
            slot = rows.at[block_of(c, x, zz), :, cut_in(j)]
            remote(slot, slot, zs.at[j, zz], zr.at[j, zz], ep=zz).wait_recv()
            for xx in x_others:
                go(remote(slot, slot, xs.at[j, zz, xx], xr.at[j, zz, x], node=xx))

    def forward_pair(j):
        for zz in z_order[1:] if j else z_order:
            for xx in x_others:
                slot = rows.at[block_of(c, xx, zz), :, cut_in(j) if zz is not z_order[0] else slice(None)]
                remote(slot, slot, xs.at[j, zz, xx], xr.at[j, zz, xx], node=xx).wait_recv()
        mine = rows.at[pl.ds(c * half, half), :, cut_in(j)]
        go(remote(mine, mine, ps.at[j], pr.at[j], pair=other))

    group = min(ROW_BLOCKS_PER_DOT, blocks)

    def tiles(body):
        if blocks == group:
            body(0)
        else:
            lax.fori_loop(0, blocks // group, lambda i, _: (body(i), 0)[1], 0)

    def into(j):
        theirs = rows.at[pl.ds(other * half, half), :, cut_in(j)]
        remote(theirs, theirs, ps.at[j], pr.at[j], pair=other).wait_recv()
        for copy in weights_in[j]:
            copy.wait()

        def body(i):
            data = rows[pl.ds(i * group, group), :, cut_in(j)].astype(jnp.float32)
            data = data.reshape(group * height, GATHER_SPLIT[j] * 128).astype(jnp.bfloat16)
            for acc, weight in ((acc_gate, w_gate), (acc_up, w_up)):
                value = jnp.dot(data, weight[cut_in(j), :], preferred_element_type=jnp.float32)
                if j == 0:
                    acc[i] = value
                else:
                    acc[i] += value
        tiles(body)

    def activate():
        def body(i):
            gate = acc_gate[i]
            hidden[i] = (gate / (1.0 + jnp.exp(-gate)) * acc_up[i]).astype(jnp.bfloat16)
        tiles(body)

    def down(j):
        weights_out[j].wait()

        def body(i):
            value = jnp.dot(hidden[i], w_down[:, cut_out(j)], preferred_element_type=jnp.float32)
            part[pl.ds(i * group, group), :, cut_out(j)] = value.reshape(group, height, RETURN_SPLIT[j] * 128).astype(jnp.bfloat16)
        tiles(body)
        go(remote(part.at[pl.ds(other * half, half), :, cut_out(j)], part_in.at[:, :, cut_out(j)], ps2.at[j], pr2.at[j], pair=other))

    def sum_pair(j):
        remote(part_in.at[:, :, cut_out(j)], part_in.at[:, :, cut_out(j)], ps2.at[j], pr2.at[j], pair=other).wait_recv()
        for xx in x_others:
            here = pl.ds(xx * n_ep, n_ep)
            mine = part[pl.ds(c * half + xx * n_ep, n_ep), :, cut_out(j)].astype(jnp.float32)
            part_in[here, :, cut_out(j)] = (part_in[here, :, cut_out(j)].astype(jnp.float32) + mine).astype(jnp.bfloat16)

    def send_nodes(j):
        for xx in x_others:
            go(remote(part_in.at[pl.ds(xx * n_ep, n_ep), :, cut_out(j)], node_in.at[x, :, :, cut_out(j)],
                      xs2.at[j, xx], xr2.at[j, x], node=xx))

    def sum_nodes(j):
        for xx in x_others:
            slot = node_in.at[xx, :, :, cut_out(j)]
            remote(slot, slot, xs2.at[j, xx], xr2.at[j, xx], node=xx).wait_recv()
        if j + ahead_back < steps_out:
            send_nodes(j + ahead_back)
        total = part_in[pl.ds(x * n_ep, n_ep), :, cut_out(j)].astype(jnp.float32)
        total = total + part[pl.ds(c * half + x * n_ep, n_ep), :, cut_out(j)].astype(jnp.float32)
        for xx in x_others:
            total = total + node_in[xx, :, :, cut_out(j)].astype(jnp.float32)
        sums[:, :, cut_out(j)] = total.astype(jnp.bfloat16)
        for zz in z_order[1:]:
            go(remote(sums.at[zz, :, cut_out(j)], answers.at[z, :, cut_out(j)], zs2.at[j, zz], zr2.at[j, z], ep=zz))

    def weight_of(zz):
        named = jnp.sum(jnp.where(ids_ref[...] == zz, gates_ref[...], 0.0), axis=0, keepdims=True)
        square = (height, height)
        diagonal = lax.broadcasted_iota(jnp.int32, square, 0) == lax.broadcasted_iota(jnp.int32, square, 1)
        return jnp.sum(jnp.where(diagonal, jnp.broadcast_to(named, square), 0.0), axis=1, keepdims=True)

    def finish(j):
        total = None
        for zz in z_order:
            if zz is z_order[0]:
                value = sums[zz, :, cut_out(j)].astype(jnp.float32)
            else:
                slot = answers.at[zz, :, cut_out(j)]
                remote(slot, slot, zs2.at[j, zz], zr2.at[j, zz], ep=zz).wait_recv()
                value = answers[zz, :, cut_out(j)].astype(jnp.float32)
            share = weight_of(zz)
            value = jnp.where(share > 0.0, share * value, 0.0)
            total = value if total is None else total + value
        out_ref[:, cut_out(j)] = total.astype(jnp.bfloat16)
        outs[j].start()

    def drain():
        while sends:
            sends.pop(0).wait_send()

    own_copy.wait()
    ahead = min(GATHER_AHEAD, steps)
    for j in range(ahead):
        own_out(j)
        if j == 0:
            own_nodes()
    for copy in sum(weights_in, []) + weights_out:
        copy.start()
    ahead_back = min(RETURN_AHEAD, steps_out)
    for t in range(steps + 2):
        if t < steps:
            forward_nodes(t)
        if t + ahead < steps:
            own_out(t + ahead)
        if 0 <= t - 1 < steps:
            forward_pair(t - 1)
        if 0 <= t - 2 < steps:
            into(t - 2)
    activate()
    ids_copy.wait()
    gates_copy.wait()
    for t in range(steps_out + 1):
        if t < steps_out:
            down(t)
        if t >= 1:
            sum_pair(t - 1)
            if t - 1 < ahead_back:
                send_nodes(t - 1)
    drain()
    for t in range(steps_out + 2):
        if t < steps_out:
            sum_nodes(t)
        if t >= 2:
            finish(t - 2)
    drain()
    for copy in outs:
        copy.wait()


def solution(mesh):
    n_ep, n_node, n_pair = (mesh.shape[name] for name in ("ep", "node", "pair"))
    steps = max(len(GATHER_SPLIT), len(RETURN_SPLIT))

    def per_device(rows_in, expert_ids, gates, copy_expert, gate_slots, up_slots, down_slots):
        height, width = rows_in.shape
        units = gate_slots.shape[3]
        blocks = n_ep * n_node * n_pair
        group = min(ROW_BLOCKS_PER_DOT, blocks)
        bf16, f32 = jnp.bfloat16, jnp.float32
        dma = pltpu.SemaphoreType.DMA
        anywhere = pl.BlockSpec(memory_space=pl.ANY)
        return pl.pallas_call(
            functools.partial(kernel, (n_ep, n_node, n_pair)),
            out_shape=jax.ShapeDtypeStruct((height, width), bf16),
            in_specs=[anywhere] * 6,
            out_specs=anywhere,
            scratch_shapes=[
                pltpu.VMEM(expert_ids.T.shape, jnp.int32),
                pltpu.VMEM(gates.T.shape, f32),
                pltpu.VMEM((height, width), bf16),
                pltpu.VMEM((width, units), bf16),
                pltpu.VMEM((width, units), bf16),
                pltpu.VMEM((units, width), bf16),
                pltpu.VMEM((blocks, height, width), bf16),
                pltpu.VMEM((blocks // group, group * height, units), f32),
                pltpu.VMEM((blocks // group, group * height, units), f32),
                pltpu.VMEM((blocks // group, group * height, units), bf16),
                pltpu.VMEM((blocks, height, width), bf16),
                pltpu.VMEM((n_ep * n_node, height, width), bf16),
                pltpu.VMEM((n_node, n_ep, height, width), bf16),
                pltpu.VMEM((n_ep, height, width), bf16),
                pltpu.VMEM((n_ep, height, width), bf16),
                dma((3, steps)), dma((3,)), dma((steps,)),
                dma((steps, n_ep)), dma((steps, n_ep)),
                dma((steps, n_ep, n_node)), dma((steps, n_ep, n_node)),
                dma((steps,)), dma((steps,)),
                dma((steps,)), dma((steps,)),
                dma((steps, n_node)), dma((steps, n_node)),
                dma((steps, n_ep)), dma((steps, n_ep)),
            ],
            compiler_params=pltpu.CompilerParams(
                collective_id=0, has_side_effects=True, vmem_limit_bytes=60 * 1024 * 1024
            ),
        )(rows_in, expert_ids.T, gates.T, gate_slots, up_slots, down_slots)

    spec = P(("groups", "ep", "node", "pair"), None)
    return jax.shard_map(
        per_device,
        mesh=mesh,
        in_specs=(
            spec, spec, spec, P(),
            P("ep", None, None, ("node", "pair")),
            P("ep", None, None, ("node", "pair")),
            P("ep", None, ("node", "pair"), None),
        ),
        out_specs=spec,
        check_vma=False,
    )
```
